32 devices in a mesh: groups: 2 (over x), seq: 16 (over z, y, core).
Axes of the slice: x: 2, y: 2, z: 4, core: 2. Of those that a mesh axis runs over, the one named last changes fastest.
Arguments:
- tokens: bfloat16 [128, 5120], P(('groups', 'seq')), parts along dimension 0, may hold values from -6 to 6
- out_grad: bfloat16 [128, 5120], P(('groups', 'seq')), parts along dimension 0, may hold values from -6 to 6
- ffn_out: bfloat16 [128, 5120], P(('groups', 'seq')), parts along dimension 0, may hold values from -6 to 6
- modulation: float32 [42, 3, 5120], P('groups'), parts along dimension 0, may hold values from -3 to 3
- in_weight: bfloat16 [5120, 13824], P(None, 'seq'), may hold values from -0.078125 to 0.078125
- in_bias: float32 [13824], P('seq'), may hold values from -4 to 4
- out_weight: bfloat16 [13824, 5120], P('seq'), may hold values from -0.0546875 to 0.0546875
- frame_ids: int32 [128], P('groups'), parts along dimension 0, may hold values from 0 to 20, never falling along the last dimension, each value on 1 to 6 neighbouring positions
- frame_slot: int32 [42], P('groups'), parts along dimension 0, may hold values from 0 to 31, as said below
Outputs:
- token_grad: bfloat16 [128, 5120], P(('groups', 'seq')), parts along dimension 0
- in_weight_grad: bfloat16 [10240, 13824], P('groups', 'seq'), parts along dimension 0
- out_weight_grad: bfloat16 [27648, 5120], P(('groups', 'seq')), parts along dimension 0
- frame_grads: float32 [64, 3, 5120], P(('groups', 'seq')), parts along dimension 0
The draws below stay inside these ranges and needn't reach their ends.
There are 2 independent parts, one for each index of `groups`. The reference program is written for one: setup_inputs(seed, part) draws one part's arguments, and reference() takes and returns one part's arrays. A program takes and returns all parts, laid end to end along the dimension named above; an argument that names none is the same for every part. Nothing has to cross between parts.
Inputs may be any that keep to these rules, and one draw needn't show every extreme that they name: `frame_ids`: frames are runs of consecutive rows in order, each of 1 to 6 rows, one of exactly 6. `frame_slot`: distinct slots; the slot s belongs to index s // 2 of seq.
All inputs are finite; a program needn't handle non-finite values.
Results may differ from the reference program's by a relative error of at most 0.007.
Values may be sent and summed in bfloat16 or wider, within the bound.
A program may use at most 128 MiB of HBM per device.

```python
import math
import jax
import jax.numpy as jnp
import numpy as np
from jax import lax

D = 5120
FF = 13824
FRAMES = 21
TOKENS = 64
FRAME_MOST = 6
SLOTS = 32


def draw_frame_slot(key, part):
    key = jax.random.fold_in(key, 7)
    first_key, second_key = jax.random.split(key)
    others = jax.random.permutation(first_key, SLOTS - 1)[:FRAMES - 1].astype(jnp.int32)
    chosen = jnp.concatenate([others, jnp.full((1,), SLOTS - 1, jnp.int32)])
    order = jax.random.permutation(second_key, FRAMES)
    return chosen[order].astype(jnp.int32)


def block_levels(key, dims, cuts, low, largest):
    def one(position, shards_of):
        draws = jax.random.uniform(jax.random.fold_in(jax.random.fold_in(key, 6), position), (shards_of,), jnp.float32, low / len(cuts), largest / len(cuts))
        return jnp.repeat(jnp.exp(draws), dims[position] // shards_of).reshape((-1,) + (1,) * (len(dims) - position - 1))

    gain = one(*cuts[0])
    for cut in cuts[1:]:
        gain = gain * one(*cut)
    return gain


def split_up(number_of, total, limit, lean):
    loads = [(1 << 20) // math.isqrt(standing ** lean) + 1 for standing in range(2, number_of + 1)]
    spare, counts = total - limit - (number_of - 1), [1] * (number_of - 1)
    while spare > 0:
        free = [i for i in range(number_of - 1) if counts[i] < limit]
        pool, remaining = sum([loads[i] for i in free]), spare
        for i in free:
            addition = min(limit - counts[i], max(1, remaining * loads[i] // pool), spare)
            counts[i] = counts[i] + addition
            spare = spare - addition
    return np.array([limit] + counts)


def uneven(own_key, number_of, total, reach, lean):
    if number_of == 2:
        one = jax.random.randint(own_key, (), max(1, total - reach), min(reach, total - 1) + 1)
        return jnp.stack([one, total - one])
    tallies = jnp.asarray(split_up(number_of, total, reach, lean), jnp.int32)
    pairs = (number_of - 1) // 2
    giver, sink = tallies[1:1 + 2 * pairs:2], tallies[2:2 + 2 * pairs:2]
    room = jnp.minimum(giver - 1, reach - sink)
    moved = jax.random.randint(jax.random.fold_in(own_key, 1), (pairs,), 0, 1 << 20) % (room + 1)
    tallies = tallies.at[1:1 + 2 * pairs:2].set(giver - moved).at[2:2 + 2 * pairs:2].set(sink + moved)
    return tallies[jax.random.permutation(jax.random.fold_in(own_key, 2), number_of)]


def gaussian(own_key, extent, scale, bound, pieces=(), held_as=jnp.bfloat16):
    gain = block_levels(own_key, extent, pieces, -0.22, 0.18) if pieces else 1.0
    drawn = jax.random.normal(own_key, extent, jnp.float32) * scale * gain
    return jnp.minimum(jnp.maximum(drawn, -bound), bound).astype(held_as)


def setup_inputs(seed: int = 0, part: int = 0) -> dict:
    seeds = jax.random.split(jax.random.key(seed), 10)
    part_keys = jax.random.split(jax.random.fold_in(seeds[9], part), 10)
    tokens = gaussian(part_keys[0], (TOKENS, D), 1.0, 6.0, ((0, 16),))
    out_grad = gaussian(part_keys[1], (TOKENS, D), 1.0, 6.0, ((0, 16),))
    ffn_out = gaussian(part_keys[2], (TOKENS, D), 1.0, 6.0, ((0, 16),))
    modulation = gaussian(part_keys[3], (FRAMES, 3, D), 0.5, 3.0, (), jnp.float32)
    in_weight = gaussian(seeds[4], (D, FF), D ** -0.5, 0.078125, ((1, 16),))
    in_bias = gaussian(seeds[5], (FF,), 1.0, 4.0, ((0, 16),), jnp.float32)
    out_weight = gaussian(seeds[6], (FF, D), FF ** -0.5, 0.0546875, ((0, 16),))
    frame_ids = jnp.searchsorted(jnp.cumsum(uneven(part_keys[7], FRAMES, TOKENS, FRAME_MOST, 1)), jnp.arange(TOKENS), side="right").astype(jnp.int32)
    frame_slot = draw_frame_slot(jax.random.fold_in(jax.random.fold_in(seeds[9], part), 71), part)
    return {"tokens": tokens, "out_grad": out_grad, "ffn_out": ffn_out, "modulation": modulation, "in_weight": in_weight, "in_bias": in_bias, "out_weight": out_weight, "frame_ids": frame_ids, "frame_slot": frame_slot}


EPSILON = 1e-06
HIGH = lax.Precision.HIGHEST

def gelu_tanh(value_in):
    return jax.nn.gelu(value_in, approximate=True)

def normalize(inputs):
    values = inputs.astype(jnp.float32)
    centred = values - lax.optimization_barrier(jnp.mean(values, axis=1, keepdims=True))
    inverse_std = lax.rsqrt(lax.optimization_barrier(jnp.mean(centred * centred, axis=1, keepdims=True)) + EPSILON)
    return (centred * inverse_std, inverse_std)

def frame_rows(frame_index, modulation):
    frame_count = modulation.shape[0]
    one_hot = (frame_index[:, None] == jnp.arange(frame_count, dtype=jnp.int32)[None, :]).astype(jnp.float32)
    shift = jnp.dot(one_hot, modulation[:, 0, :], precision=HIGH)
    scale = jnp.dot(one_hot, modulation[:, 1, :], precision=HIGH)
    gate = jnp.dot(one_hot, modulation[:, 2, :], precision=HIGH)
    return (one_hot, shift, scale, gate)

def finish(mod_grad, normed, inverse_std, scale, out_grad):
    normed_grad = mod_grad * (1.0 + scale)
    mean_grad = lax.optimization_barrier(jnp.mean(normed_grad, axis=1, keepdims=True))
    mean_proj = lax.optimization_barrier(jnp.mean(normed_grad * normed, axis=1, keepdims=True))
    result = out_grad.astype(jnp.float32) + (normed_grad - mean_grad - normed * mean_proj) * inverse_std
    return result.astype(jnp.bfloat16)

def reference(tokens, out_grad, ffn_out, modulation, in_weight, in_bias, out_weight, frame_ids, frame_slot):
    one_hot, shift, scale, gate = frame_rows(frame_ids, modulation)
    normed, inverse_std = normalize(tokens)
    modulated = (normed * (1.0 + scale) + shift).astype(jnp.bfloat16)
    gated_grad = (out_grad.astype(jnp.float32) * gate).astype(jnp.bfloat16)
    hidden_pre = jnp.dot(modulated, in_weight, preferred_element_type=jnp.float32) + in_bias
    activated, pull_back = jax.vjp(gelu_tanh, hidden_pre)
    activated = activated.astype(jnp.bfloat16)
    out_weight_grad = jnp.dot(activated.T, gated_grad, preferred_element_type=jnp.float32).astype(jnp.bfloat16)
    act_grad = jnp.dot(gated_grad, out_weight.T, preferred_element_type=jnp.float32)
    hidden_grad = pull_back(act_grad)[0].astype(jnp.bfloat16)
    in_weight_grad = jnp.dot(modulated.T, hidden_grad, preferred_element_type=jnp.float32).astype(jnp.bfloat16)
    mod_grad = jnp.dot(hidden_grad, in_weight.T, preferred_element_type=jnp.float32)
    token_grad = finish(mod_grad, normed, inverse_std, scale, out_grad)
    stacked = jnp.concatenate([mod_grad, mod_grad * normed, out_grad.astype(jnp.float32) * ffn_out.astype(jnp.float32)], axis=1)
    per_frame = jnp.dot(one_hot.T, stacked, precision=HIGH)
    slot_hot = (frame_slot[:, None] == jnp.arange(SLOTS, dtype=jnp.int32)[None, :]).astype(jnp.float32)
    frame_grads = jnp.dot(slot_hot.T, per_frame, precision=HIGH).reshape(SLOTS, 3, D)
    return (token_grad, in_weight_grad, out_weight_grad, frame_grads)
```

```python
import functools

import jax
import jax.numpy as jnp
import numpy as np
from jax import lax
from jax.experimental import pallas as pl
from jax.experimental.pallas import tpu as pltpu
from jax.sharding import PartitionSpec as P

EPSILON = 1e-06
MESH = pl.DeviceIdType.MESH


def gelu_tanh(value_in):
    return jax.nn.gelu(value_in, approximate=True)


def normalize(inputs):
    values = inputs.astype(jnp.float32)
    centred = values - jnp.mean(values, axis=1, keepdims=True)
    inverse_std = lax.rsqrt(jnp.mean(centred * centred, axis=1, keepdims=True) + EPSILON)
    return (centred * inverse_std, inverse_std)


def position(lines):
    me = lax.axis_index("seq")
    return me, me // 4, (me // 2) % 2, me % 2


def device(line, side, core):
    return {"seq": (line * 2 + side) * 2 + core}


def greet(lines, line, side, core):
    barrier = pltpu.get_barrier_semaphore()
    for step in range(1, lines):
        pl.semaphore_signal(
            barrier, inc=1, device_id=device((line + step) % lines, side, core), device_id_type=MESH
        )
    pl.semaphore_signal(barrier, inc=1, device_id=device(line, 1 - side, core), device_id_type=MESH)
    pl.semaphore_signal(barrier, inc=1, device_id=device(line, side, 1 - core), device_id_type=MESH)
    pl.semaphore_wait(barrier, lines + 1)


def gather_kernel(lines, mine_ref, all_ref, line_send, side_send, core_send, recv):
    me, line, side, core = position(lines)
    greet(lines, line, side, core)

    def copy(source, block, send, where):
        return pltpu.make_async_remote_copy(
            src_ref=source,
            dst_ref=all_ref.at[block],
            send_sem=send,
            recv_sem=recv.at[block],
            device_id=where,
            device_id_type=MESH,
        )

    def arrived(block):
        copy(all_ref.at[block], block, line_send.at[0], device(line, side, 1 - core)).wait_recv()

    sent = []

    def send(source, block, sem, where):
        started = copy(source, block, sem, where)
        started.start()
        sent.append(started)

    for step in range(1, lines):
        send(mine_ref, me, line_send.at[step - 1], device((line + step) % lines, side, core))
    send(mine_ref, me, side_send.at[0], device(line, 1 - side, core))
    send(mine_ref, me, core_send.at[0], device(line, side, 1 - core))
    all_ref[me] = mine_ref[...]
    for step in range(1, lines):
        block = (((line - step + lines) % lines) * 2 + side) * 2 + core
        arrived(block)
        send(all_ref.at[block], block, side_send.at[step], device(line, 1 - side, core))
        send(all_ref.at[block], block, core_send.at[step], device(line, side, 1 - core))
    for step in range(lines):
        block = (((line - step + lines) % lines) * 2 + 1 - side) * 2 + core
        arrived(block)
        send(all_ref.at[block], block, core_send.at[lines + step], device(line, side, 1 - core))
    for step in range(lines):
        for other in range(2):
            arrived((((line - step + lines) % lines) * 2 + other) * 2 + 1 - core)
    for started in sent:
        started.wait_send()


def gather_blocks(block, n):
    lines = n // 4
    return pl.pallas_call(
        functools.partial(gather_kernel, lines),
        out_shape=jax.ShapeDtypeStruct((n,) + block.shape, block.dtype),
        in_specs=[pl.BlockSpec(memory_space=pltpu.VMEM)],
        out_specs=pl.BlockSpec(memory_space=pltpu.VMEM),
        scratch_shapes=[
            pltpu.SemaphoreType.DMA((lines,)),
            pltpu.SemaphoreType.DMA((lines,)),
            pltpu.SemaphoreType.DMA((2 * lines,)),
            pltpu.SemaphoreType.DMA((n,)),
        ],
        compiler_params=pltpu.CompilerParams(
            collective_id=0, has_side_effects=True, vmem_limit_bytes=32 * 2**20
        ),
        name="gather_rows",
    )(block)


def reduce_kernel(
    lines,
    parts_ref,
    out_ref,
    from_core,
    to_side,
    from_side,
    to_line,
    from_line,
    core_send,
    core_recv,
    side_send,
    side_recv,
    line_send,
    line_recv,
):
    me, line, side, core = position(lines)
    greet(lines, line, side, core)
    sent = []

    def send(source, target, send_sem, recv_sem, where):
        started = pltpu.make_async_remote_copy(
            src_ref=source,
            dst_ref=target,
            send_sem=send_sem,
            recv_sem=recv_sem,
            device_id=where,
            device_id_type=MESH,
        )
        started.start()
        sent.append(started)
        return started

    order = [(line + step) % lines for step in list(range(1, lines)) + [0]]
    core_copies = {}
    for away in (1, 0):
        for step, place in enumerate(order):
            other = 1 - side if away else side
            slot = away * lines + step
            core_copies[slot] = send(
                parts_ref.at[1 - core, other, place],
                from_core.at[slot],
                core_send.at[slot],
                core_recv.at[slot],
                device(line, side, 1 - core),
            )
    side_copies = []
    for step, place in enumerate(order):
        slot = lines + step
        core_copies[slot].wait_recv()
        to_side[step] = (
            parts_ref[core, 1 - side, place].astype(jnp.float32)
            + from_core[slot].astype(jnp.float32)
        ).astype(jnp.bfloat16)
        side_copies.append(
            send(
                to_side.at[step],
                from_side.at[step],
                side_send.at[step],
                side_recv.at[step],
                device(line, 1 - side, core),
            )
        )
    line_copies = []
    for step, place in enumerate(order):
        core_copies[step].wait_recv()
        side_copies[step].wait_recv()
        total = (
            parts_ref[core, side, place].astype(jnp.float32)
            + from_core[step].astype(jnp.float32)
            + from_side[step].astype(jnp.float32)
        )
        if step < lines - 1:
            to_line[step] = total.astype(jnp.bfloat16)
            line_copies.append(
                send(
                    to_line.at[step],
                    from_line.at[step],
                    line_send.at[step],
                    line_recv.at[step],
                    device(place, side, core),
                )
            )
        else:
            out_ref[...] = total
    for step in range(lines - 1):
        line_copies[step].wait_recv()
        out_ref[...] += from_line[step].astype(jnp.float32)
    for started in sent:
        started.wait_send()


def reduce_blocks(parts, n):
    lines = n // 4
    block = parts.shape[3:]
    return pl.pallas_call(
        functools.partial(reduce_kernel, lines),
        out_shape=jax.ShapeDtypeStruct(block, jnp.float32),
        in_specs=[pl.BlockSpec(memory_space=pltpu.VMEM)],
        out_specs=pl.BlockSpec(memory_space=pltpu.VMEM),
        scratch_shapes=[
            pltpu.VMEM((2 * lines,) + block, jnp.bfloat16),
            pltpu.VMEM((lines,) + block, jnp.bfloat16),
            pltpu.VMEM((lines,) + block, jnp.bfloat16),
            pltpu.VMEM((lines,) + block, jnp.bfloat16),
            pltpu.VMEM((lines,) + block, jnp.bfloat16),
            pltpu.SemaphoreType.DMA((2 * lines,)),
            pltpu.SemaphoreType.DMA((2 * lines,)),
            pltpu.SemaphoreType.DMA((lines,)),
            pltpu.SemaphoreType.DMA((lines,)),
            pltpu.SemaphoreType.DMA((lines,)),
            pltpu.SemaphoreType.DMA((lines,)),
        ],
        compiler_params=pltpu.CompilerParams(
            collective_id=1, has_side_effects=True, vmem_limit_bytes=32 * 2**20
        ),
        name="reduce_rows",
    )(parts)


def finish(mod_grad, normed, inverse_std, scale, out_grad):
    normed_grad = mod_grad * (1.0 + scale)
    mean_grad = jnp.mean(normed_grad, axis=1, keepdims=True)
    mean_proj = jnp.mean(normed_grad * normed, axis=1, keepdims=True)
    result = (
        out_grad.astype(jnp.float32) + (normed_grad - mean_grad - normed * mean_proj) * inverse_std
    )
    return result.astype(jnp.bfloat16)


def per_device(
    tokens, out_grad, ffn_out, modulation, in_weight, in_bias, out_weight, frame_ids, frame_slot
):
    rows, features = tokens.shape
    frame_count = modulation.shape[0]
    n = lax.axis_size("seq")
    lines = n // 4
    total_rows = rows * n
    half = features // 2
    row_base = lax.axis_index("seq") * rows

    one_hot = frame_ids[:, None] == jnp.arange(frame_count, dtype=jnp.int32)[None, :]
    row_slot = jnp.sum(jnp.where(one_hot, frame_slot[None, :], 0), axis=1)
    one_hot = one_hot.astype(jnp.float32)

    def spread(which):
        return jnp.dot(one_hot, modulation[:, which, :], precision=lax.Precision.HIGH)

    shift, scale, gate = spread(0), spread(1), spread(2)

    mine = jnp.concatenate([tokens[:, :half], out_grad[:, :half], tokens[:, half:], out_grad[:, half:]], axis=0)
    gathered = gather_blocks(mine, n).reshape(n, 2, 2, rows, half)

    def whole(which):
        return jnp.concatenate(
            [gathered[:, side, which].reshape(total_rows, half) for side in range(2)], axis=1
        )

    all_tokens, all_out_grad = whole(0), whole(1)
    normed, inverse_std = normalize(all_tokens)
    modulated = (normed * (1.0 + scale) + shift).astype(jnp.bfloat16)
    gated_grad = (all_out_grad.astype(jnp.float32) * gate).astype(jnp.bfloat16)

    hidden_pre = jnp.dot(modulated, in_weight, preferred_element_type=jnp.float32) + in_bias
    activated, pull_back = jax.vjp(gelu_tanh, hidden_pre)
    activated = activated.astype(jnp.bfloat16)
    act_grad = lax.dot_general(
        gated_grad, out_weight, (((1,), (1,)), ((), ())), preferred_element_type=jnp.float32
    )
    hidden_grad = pull_back(act_grad)[0].astype(jnp.bfloat16)
    partial = lax.dot_general(
        hidden_grad, in_weight, (((1,), (1,)), ((), ())), preferred_element_type=jnp.float32
    )

    per_owner = (frame_count + n - 1) // n
    kinds = rows + 3 * per_owner
    kinds += kinds % 2
    owner = np.arange(n).reshape(lines, 2, 2).transpose(2, 1, 0).reshape(n, 1)
    token_of = np.full((n, kinds), -1, np.int32)
    token_of[:, :rows] = owner * rows + np.arange(rows)
    slot_of = np.full((3, n, kinds), -1, np.int32)
    for kind in range(3):
        first = rows + kind * per_owner
        slot_of[kind, :, first : first + per_owner] = owner * per_owner + np.arange(per_owner)
    token_of = token_of.reshape(-1, 1)
    slot_of = slot_of.reshape(3, -1, 1)
    my_slot = lax.dynamic_slice_in_dim(row_slot, row_base, rows, 0)
    choose = jnp.concatenate(
        [
            (token_of == np.arange(total_rows, dtype=np.int32)[None, :])
            | (slot_of[0] == row_slot[None, :]),
            slot_of[1] == row_slot[None, :],
            slot_of[2] == my_slot[None, :],
        ],
        axis=1,
    ).astype(jnp.bfloat16)
    gate_rows = out_grad.astype(jnp.float32) * ffn_out.astype(jnp.float32)
    terms = jnp.concatenate(
        [
            partial.astype(jnp.bfloat16),
            (partial * normed).astype(jnp.bfloat16),
            gate_rows.astype(jnp.bfloat16),
        ],
        axis=0,
    )
    parts = jnp.dot(choose, terms, preferred_element_type=jnp.float32).astype(jnp.bfloat16)
    cuts = 8
    parts = parts.reshape(2, 2, lines, kinds, cuts, features // cuts).transpose(0, 1, 2, 4, 3, 5)
    parts = parts.reshape(2, 2, lines, cuts * kinds, features // cuts)
    sums = reduce_blocks(parts, n)
    sums = sums.reshape(cuts, kinds, features // cuts).transpose(1, 0, 2).reshape(kinds, features)

    out_weight_grad = jnp.einsum(
        "tf,td->fd", activated, gated_grad, preferred_element_type=jnp.float32
    ).astype(jnp.bfloat16)
    in_weight_grad = jnp.einsum(
        "td,tf->df", modulated, hidden_grad, preferred_element_type=jnp.float32
    ).astype(jnp.bfloat16)

    mod_grad = sums[:rows]
    my_scale = lax.dynamic_slice_in_dim(scale, row_base, rows, 0)
    my_normed, my_inverse_std = normalize(tokens)
    token_grad = finish(mod_grad, my_normed, my_inverse_std, my_scale, out_grad)
    frame_grads = sums[rows : rows + 3 * per_owner].reshape(3, per_owner, features)
    return (token_grad, in_weight_grad, out_weight_grad, frame_grads.transpose(1, 0, 2))


def solution(mesh):
    in_specs = (
        P(("groups", "seq"), None),
        P(("groups", "seq"), None),
        P(("groups", "seq"), None),
        P("groups", None, None),
        P(None, "seq"),
        P("seq"),
        P("seq", None),
        P("groups"),
        P("groups"),
    )
    out_specs = (
        P(("groups", "seq"), None),
        P("groups", "seq"),
        P(("groups", "seq"), None),
        P(("groups", "seq"), None, None),
    )
    return jax.shard_map(
        per_device, mesh=mesh, in_specs=in_specs, out_specs=out_specs, check_vma=False
    )
```

```python
import functools

import jax
import jax.numpy as jnp
import numpy as np
from jax import lax
from jax.experimental import pallas as pl
from jax.experimental.pallas import tpu as pltpu
from jax.sharding import PartitionSpec as P

EPSILON = 1e-06
MESH = pl.DeviceIdType.MESH


def gelu_tanh(value_in):
    return jax.nn.gelu(value_in, approximate=True)


def normalize(inputs):
    values = inputs.astype(jnp.float32)
    centred = values - jnp.mean(values, axis=1, keepdims=True)
    inverse_std = lax.rsqrt(jnp.mean(centred * centred, axis=1, keepdims=True) + EPSILON)
    return (centred * inverse_std, inverse_std)


def position(lines):
    me = lax.axis_index("seq")
    return me, me // 4, (me // 2) % 2, me % 2


def device(line, side, core):
    return {"seq": (line * 2 + side) * 2 + core}


def greet(lines, line, side, core):
    barrier = pltpu.get_barrier_semaphore()
    for step in range(1, lines):
        pl.semaphore_signal(
            barrier, inc=1, device_id=device((line + step) % lines, side, core), device_id_type=MESH
        )
    pl.semaphore_signal(barrier, inc=1, device_id=device(line, 1 - side, core), device_id_type=MESH)
    pl.semaphore_signal(barrier, inc=1, device_id=device(line, side, 1 - core), device_id_type=MESH)
    pl.semaphore_wait(barrier, lines + 1)


def gather_kernel(lines, pieces, mine_ref, all_ref, line_send, side_send, core_send, recv):
    me, line, side, core = position(lines)
    greet(lines, line, side, core)
    sent = []

    def copy(source, block, piece, send, where):
        return pltpu.make_async_remote_copy(
            src_ref=source,
            dst_ref=all_ref.at[block, piece],
            send_sem=send.at[piece],
            recv_sem=recv.at[block, piece],
            device_id=where,
            device_id_type=MESH,
        )

    def arrived(block, piece):
        copy(
            all_ref.at[block, piece], block, piece, core_send.at[0], device(line, side, 1 - core)
        ).wait_recv()

    def send(source, block, piece, sem, where):
        started = copy(source, block, piece, sem, where)
        started.start()
        sent.append(started)

    for piece in range(pieces):
        for step in range(1, lines):
            send(
                mine_ref.at[piece],
                me,
                piece,
                line_send.at[step - 1],
                device((line + step) % lines, side, core),
            )
        send(mine_ref.at[piece], me, piece, side_send.at[0], device(line, 1 - side, core))
        send(mine_ref.at[piece], me, piece, core_send.at[0], device(line, side, 1 - core))
    all_ref[me] = mine_ref[...]

    def across(piece):
        for step in range(lines):
            block = (((line - step + lines) % lines) * 2 + 1 - side) * 2 + core
            arrived(block, piece)
            send(
                all_ref.at[block, piece],
                block,
                piece,
                core_send.at[lines + step],
                device(line, side, 1 - core),
            )

    for piece in range(pieces):
        for step in range(1, lines):
            block = (((line - step + lines) % lines) * 2 + side) * 2 + core
            arrived(block, piece)
            source = all_ref.at[block, piece]
            send(source, block, piece, side_send.at[step], device(line, 1 - side, core))
            send(source, block, piece, core_send.at[step], device(line, side, 1 - core))
        if piece:
            across(piece - 1)
    across(pieces - 1)
    for piece in range(pieces):
        for step in range(lines):
            for other in range(2):
                arrived((((line - step + lines) % lines) * 2 + other) * 2 + 1 - core, piece)
    for started in sent:
        started.wait_send()


def gather_blocks(block, n):
    lines, pieces = n // 4, block.shape[0]
    return pl.pallas_call(
        functools.partial(gather_kernel, lines, pieces),
        out_shape=jax.ShapeDtypeStruct((n,) + block.shape, block.dtype),
        in_specs=[pl.BlockSpec(memory_space=pltpu.VMEM)],
        out_specs=pl.BlockSpec(memory_space=pltpu.VMEM),
        scratch_shapes=[
            pltpu.SemaphoreType.DMA((lines, pieces)),
            pltpu.SemaphoreType.DMA((lines, pieces)),
            pltpu.SemaphoreType.DMA((2 * lines, pieces)),
            pltpu.SemaphoreType.DMA((n, pieces)),
        ],
        compiler_params=pltpu.CompilerParams(
            collective_id=0, has_side_effects=True, vmem_limit_bytes=8 * 2**20
        ),
        name="gather_rows",
    )(block)


def reduce_kernel(
    lines,
    parts_ref,
    out_ref,
    from_core,
    to_side,
    from_side,
    to_line,
    from_line,
    core_send,
    core_recv,
    side_send,
    side_recv,
    line_send,
    line_recv,
):
    me, line, side, core = position(lines)
    greet(lines, line, side, core)
    sent = []

    def send(source, target, send_sem, recv_sem, where):
        started = pltpu.make_async_remote_copy(
            src_ref=source,
            dst_ref=target,
            send_sem=send_sem,
            recv_sem=recv_sem,
            device_id=where,
            device_id_type=MESH,
        )
        started.start()
        sent.append(started)
        return started

    order = [(line + step) % lines for step in list(range(1, lines)) + [0]]
    core_copies = {}
    for away in (1, 0):
        for step, place in enumerate(order):
            other = 1 - side if away else side
            slot = away * lines + step
            core_copies[slot] = send(
                parts_ref.at[1 - core, other, place],
                from_core.at[slot],
                core_send.at[slot],
                core_recv.at[slot],
                device(line, side, 1 - core),
            )
    side_copies = []
    for step, place in enumerate(order):
        slot = lines + step
        core_copies[slot].wait_recv()
        to_side[step] = (
            parts_ref[core, 1 - side, place].astype(jnp.float32)
            + from_core[slot].astype(jnp.float32)
        ).astype(jnp.bfloat16)
        side_copies.append(
            send(
                to_side.at[step],
                from_side.at[step],
                side_send.at[step],
                side_recv.at[step],
                device(line, 1 - side, core),
            )
        )
    line_copies = []
    for step, place in enumerate(order):
        core_copies[step].wait_recv()
        side_copies[step].wait_recv()
        total = (
            parts_ref[core, side, place].astype(jnp.float32)
            + from_core[step].astype(jnp.float32)
            + from_side[step].astype(jnp.float32)
        )
        if step < lines - 1:
            to_line[step] = total.astype(jnp.bfloat16)
            line_copies.append(
                send(
                    to_line.at[step],
                    from_line.at[step],
                    line_send.at[step],
                    line_recv.at[step],
                    device(place, side, core),
                )
            )
        else:
            out_ref[...] = total
    for step in range(lines - 1):
        line_copies[step].wait_recv()
        out_ref[...] += from_line[step].astype(jnp.float32)
    for started in sent:
        started.wait_send()


def reduce_blocks(parts, n):
    lines = n // 4
    block = parts.shape[3:]
    return pl.pallas_call(
        functools.partial(reduce_kernel, lines),
        out_shape=jax.ShapeDtypeStruct(block, jnp.float32),
        in_specs=[pl.BlockSpec(memory_space=pltpu.VMEM)],
        out_specs=pl.BlockSpec(memory_space=pltpu.VMEM),
        scratch_shapes=[
            pltpu.VMEM((2 * lines,) + block, jnp.bfloat16),
            pltpu.VMEM((lines,) + block, jnp.bfloat16),
            pltpu.VMEM((lines,) + block, jnp.bfloat16),
            pltpu.VMEM((lines,) + block, jnp.bfloat16),
            pltpu.VMEM((lines,) + block, jnp.bfloat16),
            pltpu.SemaphoreType.DMA((2 * lines,)),
            pltpu.SemaphoreType.DMA((2 * lines,)),
            pltpu.SemaphoreType.DMA((lines,)),
            pltpu.SemaphoreType.DMA((lines,)),
            pltpu.SemaphoreType.DMA((lines,)),
            pltpu.SemaphoreType.DMA((lines,)),
        ],
        compiler_params=pltpu.CompilerParams(
            collective_id=1, has_side_effects=True, vmem_limit_bytes=20 * 2**20
        ),
        name="reduce_rows",
    )(parts)


def product_kernel(activated_ref, gated_ref, hidden_ref, modulated_ref, out_ref, in_ref):
    for left_ref, right_ref, target_ref in (
        (activated_ref, gated_ref, out_ref),
        (hidden_ref, modulated_ref, in_ref),
    ):
        target_ref[...] = lax.dot_general(
            left_ref[...],
            right_ref[...],
            (((0,), (0,)), ((), ())),
            preferred_element_type=jnp.float32,
        ).astype(jnp.bfloat16)


def weight_products(activated, gated_grad, hidden_grad, modulated):
    (total_rows, hidden), features = activated.shape, modulated.shape[1]
    width = 512
    left = pl.BlockSpec((total_rows, hidden), lambda index: (0, 0))
    right = pl.BlockSpec((total_rows, width), lambda index: (0, index))
    target = pl.BlockSpec((hidden, width), lambda index: (0, index))
    shape = jax.ShapeDtypeStruct((hidden, features), jnp.bfloat16)
    return pl.pallas_call(
        product_kernel,
        grid=(features // width,),
        out_shape=(shape, shape),
        in_specs=[left, right, left, right],
        out_specs=(target, target),
        compiler_params=pltpu.CompilerParams(vmem_limit_bytes=24 * 2**20),
        name="weight_products",
    )(activated, gated_grad, hidden_grad, modulated)


def finish(mod_grad, normed, inverse_std, scale, out_grad):
    normed_grad = mod_grad * (1.0 + scale)
    mean_grad = jnp.mean(normed_grad, axis=1, keepdims=True)
    mean_proj = jnp.mean(normed_grad * normed, axis=1, keepdims=True)
    result = (
        out_grad.astype(jnp.float32) + (normed_grad - mean_grad - normed * mean_proj) * inverse_std
    )
    return result.astype(jnp.bfloat16)


def per_device(
    tokens, out_grad, ffn_out, modulation, in_weight, in_bias, out_weight, frame_ids, frame_slot
):
    rows, features = tokens.shape
    frame_count = modulation.shape[0]
    n = lax.axis_size("seq")
    lines = n // 4
    total_rows = rows * n
    half = features // 2
    pieces = 4
    row_base = lax.axis_index("seq") * rows

    one_hot = frame_ids[:, None] == jnp.arange(frame_count, dtype=jnp.int32)[None, :]
    row_slot = jnp.sum(jnp.where(one_hot, frame_slot[None, :], 0), axis=1)
    one_hot = one_hot.astype(jnp.float32)

    def spread(which):
        return jnp.dot(one_hot, modulation[:, which, :], precision=lax.Precision.HIGH)

    shift, scale, gate = spread(0), spread(1), spread(2)

    mine = jnp.concatenate([tokens[:, :half], out_grad[:, :half], tokens[:, half:], out_grad[:, half:]], axis=0)
    mine = mine.reshape(4 * rows, pieces, half // pieces).transpose(1, 0, 2)
    gathered = gather_blocks(mine, n).transpose(0, 2, 1, 3).reshape(n, 2, 2, rows, half)

    def whole(which):
        return jnp.concatenate(
            [gathered[:, side, which].reshape(total_rows, half) for side in range(2)], axis=1
        )

    all_tokens, all_out_grad = whole(0), whole(1)
    normed, inverse_std = normalize(all_tokens)
    modulated = (normed * (1.0 + scale) + shift).astype(jnp.bfloat16)
    gated_grad = (all_out_grad.astype(jnp.float32) * gate).astype(jnp.bfloat16)

    hidden_pre = jnp.dot(modulated, in_weight, preferred_element_type=jnp.float32) + in_bias
    activated, pull_back = jax.vjp(gelu_tanh, hidden_pre)
    activated = activated.astype(jnp.bfloat16)
    act_grad = lax.dot_general(
        gated_grad, out_weight, (((1,), (1,)), ((), ())), preferred_element_type=jnp.float32
    )
    hidden_grad = pull_back(act_grad)[0].astype(jnp.bfloat16)
    partial = lax.dot_general(
        hidden_grad, in_weight, (((1,), (1,)), ((), ())), preferred_element_type=jnp.float32
    )

    per_owner = (frame_count + n - 1) // n
    kinds = rows + 3 * per_owner
    kinds += kinds % 2
    owner = np.arange(n).reshape(lines, 2, 2).transpose(2, 1, 0).reshape(n, 1)
    token_of = np.full((n, kinds), -1, np.int32)
    token_of[:, :rows] = owner * rows + np.arange(rows)
    slot_of = np.full((3, n, kinds), -1, np.int32)
    for kind in range(3):
        first = rows + kind * per_owner
        slot_of[kind, :, first : first + per_owner] = owner * per_owner + np.arange(per_owner)
    token_of = token_of.reshape(-1, 1)
    slot_of = slot_of.reshape(3, -1, 1)
    my_slot = lax.dynamic_slice_in_dim(row_slot, row_base, rows, 0)
    choose = jnp.concatenate(
        [
            (token_of == np.arange(total_rows, dtype=np.int32)[None, :])
            | (slot_of[0] == row_slot[None, :]),
            slot_of[1] == row_slot[None, :],
            slot_of[2] == my_slot[None, :],
        ],
        axis=1,
    ).astype(jnp.bfloat16)
    gate_rows = out_grad.astype(jnp.float32) * ffn_out.astype(jnp.float32)
    terms = jnp.concatenate(
        [
            partial.astype(jnp.bfloat16),
            (partial * normed).astype(jnp.bfloat16),
            gate_rows.astype(jnp.bfloat16),
        ],
        axis=0,
    )
    parts = jnp.dot(choose, terms, preferred_element_type=jnp.float32).astype(jnp.bfloat16)
    cuts = 8
    parts = parts.reshape(2, 2, lines, kinds, cuts, features // cuts).transpose(0, 1, 2, 4, 3, 5)
    parts = parts.reshape(2, 2, lines, cuts * kinds, features // cuts)
    sums = reduce_blocks(parts, n)
    sums = sums.reshape(cuts, kinds, features // cuts).transpose(1, 0, 2).reshape(kinds, features)

    out_weight_grad, in_weight_grad = weight_products(activated, gated_grad, hidden_grad, modulated)
    in_weight_grad = in_weight_grad.T

    mod_grad = sums[:rows]
    my_scale = lax.dynamic_slice_in_dim(scale, row_base, rows, 0)
    my_normed, my_inverse_std = normalize(tokens)
    token_grad = finish(mod_grad, my_normed, my_inverse_std, my_scale, out_grad)
    frame_grads = sums[rows : rows + 3 * per_owner].reshape(3, per_owner, features)
    return (token_grad, in_weight_grad, out_weight_grad, frame_grads.transpose(1, 0, 2))


def solution(mesh):
    in_specs = (
        P(("groups", "seq"), None),
        P(("groups", "seq"), None),
        P(("groups", "seq"), None),
        P("groups", None, None),
        P(None, "seq"),
        P("seq"),
        P("seq", None),
        P("groups"),
        P("groups"),
    )
    out_specs = (
        P(("groups", "seq"), None),
        P("groups", "seq"),
        P(("groups", "seq"), None),
        P(("groups", "seq"), None, None),
    )
    return jax.shard_map(
        per_device, mesh=mesh, in_specs=in_specs, out_specs=out_specs, check_vma=False
    )
```

```python
import functools

import jax
import jax.numpy as jnp
import numpy as np
from jax import lax
from jax.experimental import pallas as pl
from jax.experimental.pallas import tpu as pltpu
from jax.sharding import PartitionSpec as P

EPSILON = 1e-06
MESH = pl.DeviceIdType.MESH


def normalize(inputs):
    values = inputs.astype(jnp.float32)
    centred = values - jnp.mean(values, axis=1, keepdims=True)
    inverse_std = lax.rsqrt(jnp.mean(centred * centred, axis=1, keepdims=True) + EPSILON)
    return (centred * inverse_std, inverse_std)


def position(lines):
    me = lax.axis_index("seq")
    return me, me // 4, (me // 2) % 2, me % 2


def device(line, side, core):
    return {"seq": (line * 2 + side) * 2 + core}


def greet(lines, line, side, core):
    barrier = pltpu.get_barrier_semaphore()
    for step in range(1, lines):
        pl.semaphore_signal(
            barrier, inc=1, device_id=device((line + step) % lines, side, core), device_id_type=MESH
        )
    pl.semaphore_signal(barrier, inc=1, device_id=device(line, 1 - side, core), device_id_type=MESH)
    pl.semaphore_signal(barrier, inc=1, device_id=device(line, side, 1 - core), device_id_type=MESH)
    pl.semaphore_wait(barrier, lines + 1)


def middle_kernel(
    lines,
    mine_ref,
    pick_ref,
    ids_ref,
    modulation_ref,
    in_weight_hbm,
    bias_ref,
    out_weight_hbm,
    modulated_ref,
    gated_ref,
    activated_ref,
    hidden_ref,
    terms_ref,
    all_ref,
    in_weight_ref,
    out_weight_ref,
    tokens_ref,
    line_send,
    side_send,
    core_send,
    recv,
    load,
):
    loads = [
        pltpu.make_async_copy(in_weight_hbm, in_weight_ref, load.at[0]),
        pltpu.make_async_copy(out_weight_hbm, out_weight_ref, load.at[1]),
    ]
    for started in loads:
        started.start()
    me, line, side, core = position(lines)
    greet(lines, line, side, core)

    def copy(source, block, send, where):
        return pltpu.make_async_remote_copy(
            src_ref=source,
            dst_ref=all_ref.at[block],
            send_sem=send,
            recv_sem=recv.at[block],
            device_id=where,
            device_id_type=MESH,
        )

    def arrived(block):
        copy(all_ref.at[block], block, line_send.at[0], device(line, side, 1 - core)).wait_recv()

    sent = []

    def send(source, block, sem, where):
        started = copy(source, block, sem, where)
        started.start()
        sent.append(started)

    for step in range(1, lines):
        send(mine_ref, me, line_send.at[step - 1], device((line + step) % lines, side, core))
    send(mine_ref, me, side_send.at[0], device(line, 1 - side, core))
    send(mine_ref, me, core_send.at[0], device(line, side, 1 - core))
    all_ref[me] = mine_ref[...]
    for step in range(1, lines):
        block = (((line - step + lines) % lines) * 2 + side) * 2 + core
        arrived(block)
        send(all_ref.at[block], block, side_send.at[step], device(line, 1 - side, core))
        send(all_ref.at[block], block, core_send.at[step], device(line, side, 1 - core))
    for step in range(lines):
        block = (((line - step + lines) % lines) * 2 + 1 - side) * 2 + core
        arrived(block)
        send(all_ref.at[block], block, core_send.at[lines + step], device(line, side, 1 - core))
    for step in range(lines):
        for other in range(2):
            arrived((((line - step + lines) % lines) * 2 + other) * 2 + 1 - core)
    for started in sent:
        started.wait_send()

    n, block_rows, half = all_ref.shape
    total_rows, features = tokens_ref.shape
    width = half // 2
    flat = all_ref[...].reshape(n * block_rows, half)
    frames = lax.broadcasted_iota(jnp.int32, (total_rows, modulation_ref.shape[1]), 1)
    one_hot = (ids_ref[...] == frames).astype(jnp.float32).astype(jnp.bfloat16)

    def picked(which, column):
        place = column % half
        return jnp.dot(
            pick_ref[2 * (column // half) + which],
            flat[:, place : place + width],
            preferred_element_type=jnp.float32,
        )

    def spread(which, column):
        values = modulation_ref[which, :, column : column + width]
        high = values.astype(jnp.bfloat16)
        rest = values - high.astype(jnp.float32)
        low = rest.astype(jnp.bfloat16)
        lowest = (rest - low.astype(jnp.float32)).astype(jnp.bfloat16)
        total = jnp.dot(one_hot, lowest, preferred_element_type=jnp.float32)
        total = total + jnp.dot(one_hot, low, preferred_element_type=jnp.float32)
        return total + jnp.dot(one_hot, high, preferred_element_type=jnp.float32)

    columns = range(0, features, width)
    total = jnp.zeros((total_rows, 1), jnp.float32)
    for column in columns:
        values = picked(0, column)
        tokens_ref[:, column : column + width] = values
        total = total + jnp.sum(values, axis=1, keepdims=True)
        gated = picked(1, column) * spread(2, column)
        gated_ref[:, column : column + width] = gated.astype(jnp.bfloat16)
    mean = total / features
    total = jnp.zeros((total_rows, 1), jnp.float32)
    for column in columns:
        centred = tokens_ref[:, column : column + width] - mean
        total = total + jnp.sum(centred * centred, axis=1, keepdims=True)
    inverse_std = lax.rsqrt(total / features + EPSILON)
    for column in columns:
        normed = (tokens_ref[:, column : column + width] - mean) * inverse_std
        tokens_ref[:, column : column + width] = normed
        modulated = normed * (1.0 + spread(1, column)) + spread(0, column)
        modulated_ref[:, column : column + width] = modulated.astype(jnp.bfloat16)

    across_last = (((1,), (1,)), ((), ()))
    loads[0].wait()
    value = (
        lax.dot_general(
            modulated_ref[...],
            in_weight_ref[...],
            across_last,
            preferred_element_type=jnp.float32,
        )
        + bias_ref[...]
    )
    root = np.float32(np.sqrt(2.0 / np.pi))
    cubic = np.float32(0.044715)
    square = value * value
    bend = jnp.tanh(root * (value + cubic * (square * value)))
    activated_ref[...] = (value * (0.5 * (1.0 + bend))).astype(jnp.bfloat16)
    slope = 0.5 * (1.0 + bend) + (0.5 * value) * (1.0 - bend * bend) * (
        root * (1.0 + 3.0 * cubic * square)
    )
    loads[1].wait()
    act_grad = lax.dot_general(
        gated_ref[...], out_weight_ref[...], across_last, preferred_element_type=jnp.float32
    )
    hidden_ref[...] = (act_grad * slope).astype(jnp.bfloat16)
    for column in columns:
        partial = jnp.dot(
            hidden_ref[...],
            in_weight_ref[:, column : column + width],
            preferred_element_type=jnp.float32,
        )
        terms_ref[:total_rows, column : column + width] = partial.astype(jnp.bfloat16)
        terms_ref[total_rows:, column : column + width] = (
            partial * tokens_ref[:, column : column + width]
        ).astype(jnp.bfloat16)


def middle(block, pick, frame_ids, modulation, in_weight, in_bias, out_weight, n):
    lines = n // 4
    total_rows = frame_ids.shape[0]
    hidden, features = in_weight.shape
    vmem = pl.BlockSpec(memory_space=pltpu.VMEM)
    hbm = pl.BlockSpec(memory_space=pl.ANY)
    shapes = (
        (total_rows, features),
        (total_rows, features),
        (total_rows, hidden),
        (total_rows, hidden),
        (2 * total_rows, features),
    )
    return pl.pallas_call(
        functools.partial(middle_kernel, lines),
        out_shape=tuple(jax.ShapeDtypeStruct(shape, jnp.bfloat16) for shape in shapes),
        in_specs=[vmem, vmem, vmem, vmem, hbm, vmem, hbm],
        out_specs=(vmem,) * 5,
        scratch_shapes=[
            pltpu.VMEM((n,) + block.shape, block.dtype),
            pltpu.VMEM((hidden, features), jnp.bfloat16),
            pltpu.VMEM((hidden, features), jnp.bfloat16),
            pltpu.VMEM((total_rows, features), jnp.float32),
            pltpu.SemaphoreType.DMA((lines,)),
            pltpu.SemaphoreType.DMA((lines,)),
            pltpu.SemaphoreType.DMA((2 * lines,)),
            pltpu.SemaphoreType.DMA((n,)),
            pltpu.SemaphoreType.DMA((2,)),
        ],
        compiler_params=pltpu.CompilerParams(
            collective_id=0, has_side_effects=True, vmem_limit_bytes=56 * 2**20
        ),
        name="gather_and_middle",
    )(
        block,
        pick,
        frame_ids[:, None],
        modulation.transpose(1, 0, 2),
        in_weight,
        in_bias[None, :],
        out_weight,
    )


def reduce_kernel(
    lines,
    parts_ref,
    out_ref,
    from_core,
    to_side,
    from_side,
    to_line,
    from_line,
    core_send,
    core_recv,
    side_send,
    side_recv,
    line_send,
    line_recv,
):
    me, line, side, core = position(lines)
    greet(lines, line, side, core)
    sent = []

    def send(source, target, send_sem, recv_sem, where):
        started = pltpu.make_async_remote_copy(
            src_ref=source,
            dst_ref=target,
            send_sem=send_sem,
            recv_sem=recv_sem,
            device_id=where,
            device_id_type=MESH,
        )
        started.start()
        sent.append(started)
        return started

    order = [(line + step) % lines for step in list(range(1, lines)) + [0]]
    core_copies = {}
    for away in (1, 0):
        for step, place in enumerate(order):
            other = 1 - side if away else side
            slot = away * lines + step
            core_copies[slot] = send(
                parts_ref.at[1 - core, other, place],
                from_core.at[slot],
                core_send.at[slot],
                core_recv.at[slot],
                device(line, side, 1 - core),
            )
    side_copies = []
    for step, place in enumerate(order):
        slot = lines + step
        core_copies[slot].wait_recv()
        to_side[step] = (
            parts_ref[core, 1 - side, place].astype(jnp.float32)
            + from_core[slot].astype(jnp.float32)
        ).astype(jnp.bfloat16)
        side_copies.append(
            send(
                to_side.at[step],
                from_side.at[step],
                side_send.at[step],
                side_recv.at[step],
                device(line, 1 - side, core),
            )
        )
    line_copies = []
    for step, place in enumerate(order):
        core_copies[step].wait_recv()
        side_copies[step].wait_recv()
        total = (
            parts_ref[core, side, place].astype(jnp.float32)
            + from_core[step].astype(jnp.float32)
            + from_side[step].astype(jnp.float32)
        )
        if step < lines - 1:
            to_line[step] = total.astype(jnp.bfloat16)
            line_copies.append(
                send(
                    to_line.at[step],
                    from_line.at[step],
                    line_send.at[step],
                    line_recv.at[step],
                    device(place, side, core),
                )
            )
        else:
            out_ref[...] = total
    for step in range(lines - 1):
        line_copies[step].wait_recv()
        out_ref[...] += from_line[step].astype(jnp.float32)
    for started in sent:
        started.wait_send()


def reduce_blocks(parts, n):
    lines = n // 4
    block = parts.shape[3:]
    return pl.pallas_call(
        functools.partial(reduce_kernel, lines),
        out_shape=jax.ShapeDtypeStruct(block, jnp.float32),
        in_specs=[pl.BlockSpec(memory_space=pltpu.VMEM)],
        out_specs=pl.BlockSpec(memory_space=pltpu.VMEM),
        scratch_shapes=[
            pltpu.VMEM((2 * lines,) + block, jnp.bfloat16),
            pltpu.VMEM((lines,) + block, jnp.bfloat16),
            pltpu.VMEM((lines,) + block, jnp.bfloat16),
            pltpu.VMEM((lines,) + block, jnp.bfloat16),
            pltpu.VMEM((lines,) + block, jnp.bfloat16),
            pltpu.SemaphoreType.DMA((2 * lines,)),
            pltpu.SemaphoreType.DMA((2 * lines,)),
            pltpu.SemaphoreType.DMA((lines,)),
            pltpu.SemaphoreType.DMA((lines,)),
            pltpu.SemaphoreType.DMA((lines,)),
            pltpu.SemaphoreType.DMA((lines,)),
        ],
        compiler_params=pltpu.CompilerParams(
            collective_id=1, has_side_effects=True, vmem_limit_bytes=20 * 2**20
        ),
        name="reduce_rows",
    )(parts)


def product_kernel(activated_ref, gated_ref, hidden_ref, modulated_ref, out_ref, in_ref):
    for left_ref, right_ref, target_ref in (
        (activated_ref, gated_ref, out_ref),
        (hidden_ref, modulated_ref, in_ref),
    ):
        target_ref[...] = lax.dot_general(
            left_ref[...],
            right_ref[...],
            (((0,), (0,)), ((), ())),
            preferred_element_type=jnp.float32,
        ).astype(jnp.bfloat16)


def weight_products(activated, gated_grad, hidden_grad, modulated):
    (total_rows, hidden), features = activated.shape, modulated.shape[1]
    width = 512
    left = pl.BlockSpec((total_rows, hidden), lambda index: (0, 0))
    right = pl.BlockSpec((total_rows, width), lambda index: (0, index))
    target = pl.BlockSpec((hidden, width), lambda index: (0, index))
    shape = jax.ShapeDtypeStruct((hidden, features), jnp.bfloat16)
    return pl.pallas_call(
        product_kernel,
        grid=(features // width,),
        out_shape=(shape, shape),
        in_specs=[left, right, left, right],
        out_specs=(target, target),
        compiler_params=pltpu.CompilerParams(vmem_limit_bytes=24 * 2**20),
        name="weight_products",
    )(activated, gated_grad, hidden_grad, modulated)


def finish(mod_grad, normed, inverse_std, scale, out_grad):
    normed_grad = mod_grad * (1.0 + scale)
    mean_grad = jnp.mean(normed_grad, axis=1, keepdims=True)
    mean_proj = jnp.mean(normed_grad * normed, axis=1, keepdims=True)
    result = (
        out_grad.astype(jnp.float32) + (normed_grad - mean_grad - normed * mean_proj) * inverse_std
    )
    return result.astype(jnp.bfloat16)


def per_device(
    tokens, out_grad, ffn_out, modulation, in_weight, in_bias, out_weight, frame_ids, frame_slot
):
    rows, features = tokens.shape
    frame_count = modulation.shape[0]
    n = lax.axis_size("seq")
    lines = n // 4
    total_rows = rows * n
    half = features // 2
    row_base = lax.axis_index("seq") * rows

    one_hot = frame_ids[:, None] == jnp.arange(frame_count, dtype=jnp.int32)[None, :]
    row_slot = jnp.sum(jnp.where(one_hot, frame_slot[None, :], 0), axis=1)
    one_hot = one_hot.astype(jnp.float32)

    mine = jnp.concatenate([tokens[:, :half], out_grad[:, :half], tokens[:, half:], out_grad[:, half:]], axis=0)
    source = np.arange(total_rows) // rows * 4 * rows + np.arange(total_rows) % rows
    pick = np.stack([source + kind * rows for kind in range(4)])[:, :, None]
    pick = jnp.asarray(pick == np.arange(4 * total_rows), jnp.bfloat16)
    modulated, gated_grad, activated, hidden_grad, terms = middle(
        mine, pick, frame_ids, modulation, in_weight.T, in_bias, out_weight, n
    )

    per_owner = (frame_count + n - 1) // n
    kinds = rows + 3 * per_owner
    kinds += kinds % 2
    owner = np.arange(n).reshape(lines, 2, 2).transpose(2, 1, 0).reshape(n, 1)
    token_of = np.full((n, kinds), -1, np.int32)
    token_of[:, :rows] = owner * rows + np.arange(rows)
    slot_of = np.full((3, n, kinds), -1, np.int32)
    for kind in range(3):
        first = rows + kind * per_owner
        slot_of[kind, :, first : first + per_owner] = owner * per_owner + np.arange(per_owner)
    token_of = token_of.reshape(-1, 1)
    slot_of = slot_of.reshape(3, -1, 1)
    my_slot = lax.dynamic_slice_in_dim(row_slot, row_base, rows, 0)
    choose = jnp.concatenate(
        [
            (token_of == np.arange(total_rows, dtype=np.int32)[None, :])
            | (slot_of[0] == row_slot[None, :]),
            slot_of[1] == row_slot[None, :],
            slot_of[2] == my_slot[None, :],
        ],
        axis=1,
    ).astype(jnp.bfloat16)
    gate_rows = out_grad.astype(jnp.float32) * ffn_out.astype(jnp.float32)
    terms = jnp.concatenate(
        [
            terms,
            gate_rows.astype(jnp.bfloat16),
        ],
        axis=0,
    )
    parts = jnp.dot(choose, terms, preferred_element_type=jnp.float32).astype(jnp.bfloat16)
    cuts = 8
    parts = parts.reshape(2, 2, lines, kinds, cuts, features // cuts).transpose(0, 1, 2, 4, 3, 5)
    parts = parts.reshape(2, 2, lines, cuts * kinds, features // cuts)
    sums = reduce_blocks(parts, n)
    sums = sums.reshape(cuts, kinds, features // cuts).transpose(1, 0, 2).reshape(kinds, features)

    out_weight_grad, in_weight_grad = weight_products(activated, gated_grad, hidden_grad, modulated)
    in_weight_grad = in_weight_grad.T

    mod_grad = sums[:rows]
    my_hot = lax.dynamic_slice_in_dim(one_hot, row_base, rows, 0)
    my_scale = jnp.dot(my_hot, modulation[:, 1, :], precision=lax.Precision.HIGHEST)
    my_normed, my_inverse_std = normalize(tokens)
    token_grad = finish(mod_grad, my_normed, my_inverse_std, my_scale, out_grad)
    frame_grads = sums[rows : rows + 3 * per_owner].reshape(3, per_owner, features)
    return (token_grad, in_weight_grad, out_weight_grad, frame_grads.transpose(1, 0, 2))


def solution(mesh):
    in_specs = (
        P(("groups", "seq"), None),
        P(("groups", "seq"), None),
        P(("groups", "seq"), None),
        P("groups", None, None),
        P(None, "seq"),
        P("seq"),
        P("seq", None),
        P("groups"),
        P("groups"),
    )
    out_specs = (
        P(("groups", "seq"), None),
        P("groups", "seq"),
        P(("groups", "seq"), None),
        P(("groups", "seq"), None, None),
    )
    return jax.shard_map(
        per_device, mesh=mesh, in_specs=in_specs, out_specs=out_specs, check_vma=False
    )
```

```python
import functools

import jax
import jax.numpy as jnp
import numpy as np
from jax import lax
from jax.experimental import pallas as pl
from jax.experimental.pallas import tpu as pltpu
from jax.sharding import PartitionSpec as P

EPSILON = 1e-06
MESH = pl.DeviceIdType.MESH


def position(lines):
    me = lax.axis_index("seq")
    return me, me // 4, (me // 2) % 2, me % 2


def device(line, side, core):
    return {"seq": (line * 2 + side) * 2 + core}


def greet(lines, line, side, core):
    barrier = pltpu.get_barrier_semaphore()
    for step in range(1, lines):
        pl.semaphore_signal(
            barrier, inc=1, device_id=device((line + step) % lines, side, core), device_id_type=MESH
        )
    pl.semaphore_signal(barrier, inc=1, device_id=device(line, 1 - side, core), device_id_type=MESH)
    pl.semaphore_signal(barrier, inc=1, device_id=device(line, side, 1 - core), device_id_type=MESH)
    pl.semaphore_wait(barrier, lines + 1)


def middle_kernel(
    lines,
    mine_ref,
    pick_ref,
    one_hot_ref,
    modulation_ref,
    in_weight_hbm,
    bias_ref,
    out_weight_hbm,
    modulated_ref,
    gated_ref,
    activated_ref,
    hidden_ref,
    terms_ref,
    stats_ref,
    all_ref,
    in_weight_ref,
    out_weight_ref,
    tokens_ref,
    line_send,
    side_send,
    core_send,
    recv,
    load,
):
    loads = [
        pltpu.make_async_copy(in_weight_hbm, in_weight_ref, load.at[0]),
        pltpu.make_async_copy(out_weight_hbm, out_weight_ref, load.at[1]),
    ]
    for started in loads:
        started.start()
    me, line, side, core = position(lines)
    greet(lines, line, side, core)

    def copy(source, block, send, where):
        return pltpu.make_async_remote_copy(
            src_ref=source,
            dst_ref=all_ref.at[block],
            send_sem=send,
            recv_sem=recv.at[block],
            device_id=where,
            device_id_type=MESH,
        )

    def arrived(block):
        copy(all_ref.at[block], block, line_send.at[0], device(line, side, 1 - core)).wait_recv()

    sent = []

    def send(source, block, sem, where):
        started = copy(source, block, sem, where)
        started.start()
        sent.append(started)

    for step in range(1, lines):
        send(mine_ref, me, line_send.at[step - 1], device((line + step) % lines, side, core))
    send(mine_ref, me, side_send.at[0], device(line, 1 - side, core))
    send(mine_ref, me, core_send.at[0], device(line, side, 1 - core))
    all_ref[me] = mine_ref[...]

    half_rows = mine_ref.shape[0] // 2
    width = 2 * mine_ref.shape[1]
    own = mine_ref[...].astype(jnp.float32)
    first, second = own[:half_rows], own[half_rows:]
    own_mean = (
        jnp.sum(first, axis=1, keepdims=True) + jnp.sum(second, axis=1, keepdims=True)
    ) / width
    first, second = first - own_mean, second - own_mean
    variance = (
        jnp.sum(first * first, axis=1, keepdims=True)
        + jnp.sum(second * second, axis=1, keepdims=True)
    ) / width
    stats_ref[:half_rows] = jnp.broadcast_to(own_mean, (half_rows, 128))
    stats_ref[half_rows:] = jnp.broadcast_to(lax.rsqrt(variance + EPSILON), (half_rows, 128))

    for step in range(1, lines):
        block = (((line - step + lines) % lines) * 2 + side) * 2 + core
        arrived(block)
        send(all_ref.at[block], block, side_send.at[step], device(line, 1 - side, core))
        send(all_ref.at[block], block, core_send.at[step], device(line, side, 1 - core))
    for step in range(lines):
        block = (((line - step + lines) % lines) * 2 + 1 - side) * 2 + core
        arrived(block)
        send(all_ref.at[block], block, core_send.at[lines + step], device(line, side, 1 - core))
    for step in range(lines):
        for other in range(2):
            arrived((((line - step + lines) % lines) * 2 + other) * 2 + 1 - core)
    for started in sent:
        started.wait_send()

    n, block_rows, half = all_ref.shape
    total_rows, features = tokens_ref.shape
    width = half // 2
    flat = all_ref[...].reshape(n * block_rows, half)
    one_hot = one_hot_ref[...].astype(jnp.bfloat16)

    def picked(which, column):
        place = column % half
        return jnp.dot(
            pick_ref[2 * (column // half) + which],
            flat[:, place : place + width],
            preferred_element_type=jnp.float32,
        )

    def spread(which, column):
        values = modulation_ref[which, :, column : column + width]
        high = values.astype(jnp.bfloat16)
        rest = values - high.astype(jnp.float32)
        low = rest.astype(jnp.bfloat16)
        lowest = (rest - low.astype(jnp.float32)).astype(jnp.bfloat16)
        total = jnp.dot(one_hot, lowest, preferred_element_type=jnp.float32)
        total = total + jnp.dot(one_hot, low, preferred_element_type=jnp.float32)
        return total + jnp.dot(one_hot, high, preferred_element_type=jnp.float32)

    columns = range(0, features, width)
    total = jnp.zeros((total_rows, 1), jnp.float32)
    for column in columns:
        values = picked(0, column)
        tokens_ref[:, column : column + width] = values
        total = total + jnp.sum(values, axis=1, keepdims=True)
        gated = picked(1, column) * spread(2, column)
        gated_ref[:, column : column + width] = gated.astype(jnp.bfloat16)
    mean = total / features
    total = jnp.zeros((total_rows, 1), jnp.float32)
    for column in columns:
        centred = tokens_ref[:, column : column + width] - mean
        total = total + jnp.sum(centred * centred, axis=1, keepdims=True)
    inverse_std = lax.rsqrt(total / features + EPSILON)
    for column in columns:
        normed = (tokens_ref[:, column : column + width] - mean) * inverse_std
        tokens_ref[:, column : column + width] = normed
        modulated = normed * (1.0 + spread(1, column)) + spread(0, column)
        modulated_ref[:, column : column + width] = modulated.astype(jnp.bfloat16)

    across_last = (((1,), (1,)), ((), ()))
    loads[0].wait()
    value = (
        lax.dot_general(
            modulated_ref[...],
            in_weight_ref[...],
            across_last,
            preferred_element_type=jnp.float32,
        )
        + bias_ref[...][None, :]
    )
    root = np.float32(np.sqrt(2.0 / np.pi))
    cubic = np.float32(0.044715)
    square = value * value
    bend = jnp.tanh(root * (value + cubic * (square * value)))
    activated_ref[...] = (value * (0.5 * (1.0 + bend))).astype(jnp.bfloat16)
    slope = 0.5 * (1.0 + bend) + (0.5 * value) * (1.0 - bend * bend) * (
        root * (1.0 + 3.0 * cubic * square)
    )
    loads[1].wait()
    act_grad = lax.dot_general(
        gated_ref[...], out_weight_ref[...], across_last, preferred_element_type=jnp.float32
    )
    hidden_ref[...] = (act_grad * slope).astype(jnp.bfloat16)
    for column in columns:
        partial = jnp.dot(
            hidden_ref[...],
            in_weight_ref[:, column : column + width],
            preferred_element_type=jnp.float32,
        )
        terms_ref[:total_rows, column : column + width] = partial.astype(jnp.bfloat16)
        terms_ref[total_rows:, column : column + width] = (
            partial * tokens_ref[:, column : column + width]
        ).astype(jnp.bfloat16)


def middle(block, pick, one_hot, modulation, in_weight, in_bias, out_weight, n):
    lines = n // 4
    total_rows = one_hot.shape[0]
    hidden, features = in_weight.shape
    vmem = pl.BlockSpec(memory_space=pltpu.VMEM)
    hbm = pl.BlockSpec(memory_space=pl.ANY)
    shapes = (
        (total_rows, features),
        (total_rows, features),
        (total_rows, hidden),
        (total_rows, hidden),
        (2 * total_rows, features),
    )
    return pl.pallas_call(
        functools.partial(middle_kernel, lines),
        out_shape=tuple(jax.ShapeDtypeStruct(shape, jnp.bfloat16) for shape in shapes)
        + (jax.ShapeDtypeStruct((block.shape[0], 128), jnp.float32),),
        in_specs=[vmem, vmem, vmem, vmem, hbm, vmem, hbm],
        out_specs=(vmem,) * 6,
        scratch_shapes=[
            pltpu.VMEM((n,) + block.shape, block.dtype),
            pltpu.VMEM((hidden, features), jnp.bfloat16),
            pltpu.VMEM((hidden, features), jnp.bfloat16),
            pltpu.VMEM((total_rows, features), jnp.float32),
            pltpu.SemaphoreType.DMA((lines,)),
            pltpu.SemaphoreType.DMA((lines,)),
            pltpu.SemaphoreType.DMA((2 * lines,)),
            pltpu.SemaphoreType.DMA((n,)),
            pltpu.SemaphoreType.DMA((2,)),
        ],
        compiler_params=pltpu.CompilerParams(
            collective_id=0, has_side_effects=True, vmem_limit_bytes=56 * 2**20
        ),
        name="gather_and_middle",
    )(
        block,
        pick,
        one_hot,
        modulation.transpose(1, 0, 2),
        in_weight,
        in_bias,
        out_weight,
    )


def reduce_kernel(
    lines,
    parts_ref,
    out_ref,
    from_core,
    to_side,
    from_side,
    to_line,
    from_line,
    core_send,
    core_recv,
    side_send,
    side_recv,
    line_send,
    line_recv,
):
    me, line, side, core = position(lines)
    greet(lines, line, side, core)
    sent = []

    def send(source, target, send_sem, recv_sem, where):
        started = pltpu.make_async_remote_copy(
            src_ref=source,
            dst_ref=target,
            send_sem=send_sem,
            recv_sem=recv_sem,
            device_id=where,
            device_id_type=MESH,
        )
        started.start()
        sent.append(started)
        return started

    order = [(line + step) % lines for step in list(range(1, lines)) + [0]]
    core_copies = {}
    for away in (1, 0):
        for step, place in enumerate(order):
            other = 1 - side if away else side
            slot = away * lines + step
            core_copies[slot] = send(
                parts_ref.at[1 - core, other, place],
                from_core.at[slot],
                core_send.at[slot],
                core_recv.at[slot],
                device(line, side, 1 - core),
            )
    side_copies = []
    for step, place in enumerate(order):
        slot = lines + step
        core_copies[slot].wait_recv()
        to_side[step] = (
            parts_ref[core, 1 - side, place].astype(jnp.float32)
            + from_core[slot].astype(jnp.float32)
        ).astype(jnp.bfloat16)
        side_copies.append(
            send(
                to_side.at[step],
                from_side.at[step],
                side_send.at[step],
                side_recv.at[step],
                device(line, 1 - side, core),
            )
        )
    line_copies = []
    for step, place in enumerate(order):
        core_copies[step].wait_recv()
        side_copies[step].wait_recv()
        total = (
            parts_ref[core, side, place].astype(jnp.float32)
            + from_core[step].astype(jnp.float32)
            + from_side[step].astype(jnp.float32)
        )
        if step < lines - 1:
            to_line[step] = total.astype(jnp.bfloat16)
            line_copies.append(
                send(
                    to_line.at[step],
                    from_line.at[step],
                    line_send.at[step],
                    line_recv.at[step],
                    device(place, side, core),
                )
            )
        else:
            out_ref[...] = total
    for step in range(lines - 1):
        line_copies[step].wait_recv()
        out_ref[...] += from_line[step].astype(jnp.float32)
    for started in sent:
        started.wait_send()


def reduce_blocks(parts, n):
    lines = n // 4
    block = parts.shape[3:]
    return pl.pallas_call(
        functools.partial(reduce_kernel, lines),
        out_shape=jax.ShapeDtypeStruct(block, jnp.float32),
        in_specs=[pl.BlockSpec(memory_space=pltpu.VMEM)],
        out_specs=pl.BlockSpec(memory_space=pltpu.VMEM),
        scratch_shapes=[
            pltpu.VMEM((2 * lines,) + block, jnp.bfloat16),
            pltpu.VMEM((lines,) + block, jnp.bfloat16),
            pltpu.VMEM((lines,) + block, jnp.bfloat16),
            pltpu.VMEM((lines,) + block, jnp.bfloat16),
            pltpu.VMEM((lines,) + block, jnp.bfloat16),
            pltpu.SemaphoreType.DMA((2 * lines,)),
            pltpu.SemaphoreType.DMA((2 * lines,)),
            pltpu.SemaphoreType.DMA((lines,)),
            pltpu.SemaphoreType.DMA((lines,)),
            pltpu.SemaphoreType.DMA((lines,)),
            pltpu.SemaphoreType.DMA((lines,)),
        ],
        compiler_params=pltpu.CompilerParams(
            collective_id=1, has_side_effects=True, vmem_limit_bytes=20 * 2**20
        ),
        name="reduce_rows",
    )(parts)


def product_kernel(activated_ref, gated_ref, hidden_ref, modulated_ref, out_ref, in_ref):
    for left_ref, right_ref, target_ref in (
        (activated_ref, gated_ref, out_ref),
        (hidden_ref, modulated_ref, in_ref),
    ):
        target_ref[...] = lax.dot_general(
            left_ref[...],
            right_ref[...],
            (((0,), (0,)), ((), ())),
            preferred_element_type=jnp.float32,
        ).astype(jnp.bfloat16)


def weight_products(activated, gated_grad, hidden_grad, modulated):
    (total_rows, hidden), features = activated.shape, modulated.shape[1]
    width = 512
    left = pl.BlockSpec((total_rows, hidden), lambda index: (0, 0))
    right = pl.BlockSpec((total_rows, width), lambda index: (0, index))
    target = pl.BlockSpec((hidden, width), lambda index: (0, index))
    shape = jax.ShapeDtypeStruct((hidden, features), jnp.bfloat16)
    return pl.pallas_call(
        product_kernel,
        grid=(features // width,),
        out_shape=(shape, shape),
        in_specs=[left, right, left, right],
        out_specs=(target, target),
        compiler_params=pltpu.CompilerParams(vmem_limit_bytes=24 * 2**20),
        name="weight_products",
    )(activated, gated_grad, hidden_grad, modulated)


def finish(mod_grad, normed, inverse_std, scale, out_grad):
    normed_grad = mod_grad * (1.0 + scale)
    mean_grad = jnp.mean(normed_grad, axis=1, keepdims=True)
    mean_proj = jnp.mean(normed_grad * normed, axis=1, keepdims=True)
    result = (
        out_grad.astype(jnp.float32) + (normed_grad - mean_grad - normed * mean_proj) * inverse_std
    )
    return result.astype(jnp.bfloat16)


def per_device(
    tokens, out_grad, ffn_out, modulation, in_weight, in_bias, out_weight, frame_ids, frame_slot
):
    rows, features = tokens.shape
    frame_count = modulation.shape[0]
    n = lax.axis_size("seq")
    lines = n // 4
    total_rows = rows * n
    half = features // 2
    row_base = lax.axis_index("seq") * rows

    one_hot = frame_ids[:, None] == jnp.arange(frame_count, dtype=jnp.int32)[None, :]
    row_slot = jnp.sum(jnp.where(one_hot, frame_slot[None, :], 0), axis=1)
    one_hot = one_hot.astype(jnp.float32)

    mine = jnp.concatenate([tokens[:, :half], out_grad[:, :half], tokens[:, half:], out_grad[:, half:]], axis=0)
    source = np.arange(total_rows) // rows * 4 * rows + np.arange(total_rows) % rows
    pick = np.stack([source + kind * rows for kind in range(4)])[:, :, None]
    pick = jnp.asarray(pick == np.arange(4 * total_rows), jnp.bfloat16)
    modulated, gated_grad, activated, hidden_grad, terms, stats = middle(
        mine, pick, one_hot, modulation, in_weight.T, in_bias, out_weight, n
    )

    per_owner = (frame_count + n - 1) // n
    kinds = rows + 3 * per_owner
    kinds += kinds % 2
    owner = np.arange(n).reshape(lines, 2, 2).transpose(2, 1, 0).reshape(n, 1)
    token_of = np.full((n, kinds), -1, np.int32)
    token_of[:, :rows] = owner * rows + np.arange(rows)
    slot_of = np.full((3, n, kinds), -1, np.int32)
    for kind in range(3):
        first = rows + kind * per_owner
        slot_of[kind, :, first : first + per_owner] = owner * per_owner + np.arange(per_owner)
    token_of = token_of.reshape(-1, 1)
    slot_of = slot_of.reshape(3, -1, 1)
    my_slot = lax.dynamic_slice_in_dim(row_slot, row_base, rows, 0)
    choose = jnp.concatenate(
        [
            (token_of == np.arange(total_rows, dtype=np.int32)[None, :])
            | (slot_of[0] == row_slot[None, :]),
            slot_of[1] == row_slot[None, :],
            slot_of[2] == my_slot[None, :],
        ],
        axis=1,
    ).astype(jnp.bfloat16)
    gate_rows = out_grad.astype(jnp.float32) * ffn_out.astype(jnp.float32)
    terms = jnp.concatenate(
        [
            terms,
            gate_rows.astype(jnp.bfloat16),
        ],
        axis=0,
    )
    parts = jnp.dot(choose, terms, preferred_element_type=jnp.float32).astype(jnp.bfloat16)
    cuts = 8
    parts = parts.reshape(2, 2, lines, kinds, cuts, features // cuts).transpose(0, 1, 2, 4, 3, 5)
    parts = parts.reshape(2, 2, lines, cuts * kinds, features // cuts)
    sums = reduce_blocks(parts, n)
    sums = sums.reshape(cuts, kinds, features // cuts).transpose(1, 0, 2).reshape(kinds, features)

    out_weight_grad, in_weight_grad = weight_products(activated, gated_grad, hidden_grad, modulated)
    in_weight_grad = in_weight_grad.T

    mod_grad = sums[:rows]
    my_hot = lax.dynamic_slice_in_dim(one_hot, row_base, rows, 0)
    my_scale = jnp.dot(my_hot, modulation[:, 1, :], precision=lax.Precision.HIGHEST)
    my_inverse_std = stats[2 * rows : 3 * rows, :1]
    my_normed = (tokens.astype(jnp.float32) - stats[:rows, :1]) * my_inverse_std
    token_grad = finish(mod_grad, my_normed, my_inverse_std, my_scale, out_grad)
    frame_grads = sums[rows : rows + 3 * per_owner].reshape(3, per_owner, features)
    return (token_grad, in_weight_grad, out_weight_grad, frame_grads.transpose(1, 0, 2))


def solution(mesh):
    in_specs = (
        P(("groups", "seq"), None),
        P(("groups", "seq"), None),
        P(("groups", "seq"), None),
        P("groups", None, None),
        P(None, "seq"),
        P("seq"),
        P("seq", None),
        P("groups"),
        P("groups"),
    )
    out_specs = (
        P(("groups", "seq"), None),
        P("groups", "seq"),
        P(("groups", "seq"), None),
        P(("groups", "seq"), None, None),
    )
    return jax.shard_map(
        per_device, mesh=mesh, in_specs=in_specs, out_specs=out_specs, check_vma=False
    )
```

```python
import functools

import jax
import jax.numpy as jnp
import numpy as np
from jax import lax
from jax.experimental import pallas as pl
from jax.experimental.pallas import tpu as pltpu
from jax.sharding import PartitionSpec as P

EPSILON = 1e-06
MESH = pl.DeviceIdType.MESH


def position(lines):
    me = lax.axis_index("seq")
    return me, me // 4, (me // 2) % 2, me % 2


def device(line, side, core):
    return {"seq": (line * 2 + side) * 2 + core}


def greet(lines, line, side, core):
    barrier = pltpu.get_barrier_semaphore()
    for step in range(1, lines):
        pl.semaphore_signal(
            barrier, inc=1, device_id=device((line + step) % lines, side, core), device_id_type=MESH
        )
    pl.semaphore_signal(barrier, inc=1, device_id=device(line, 1 - side, core), device_id_type=MESH)
    pl.semaphore_signal(barrier, inc=1, device_id=device(line, side, 1 - core), device_id_type=MESH)
    pl.semaphore_wait(barrier, lines + 1)


def middle_kernel(
    lines,
    mine_ref,
    pick_ref,
    one_hot_ref,
    modulation_ref,
    in_weight_hbm,
    bias_ref,
    out_weight_hbm,
    modulated_ref,
    gated_ref,
    activated_ref,
    hidden_ref,
    terms_ref,
    stats_ref,
    all_ref,
    in_weight_ref,
    out_weight_ref,
    tokens_ref,
    rows_ref,
    line_send,
    side_send,
    core_send,
    recv,
    load,
):
    loads = [
        pltpu.make_async_copy(in_weight_hbm, in_weight_ref, load.at[0]),
        pltpu.make_async_copy(out_weight_hbm, out_weight_ref, load.at[1]),
    ]
    for started in loads:
        started.start()
    me, line, side, core = position(lines)
    greet(lines, line, side, core)

    def copy(source, block, send, where):
        return pltpu.make_async_remote_copy(
            src_ref=source,
            dst_ref=all_ref.at[block],
            send_sem=send,
            recv_sem=recv.at[block],
            device_id=where,
            device_id_type=MESH,
        )

    def arrived(block):
        copy(all_ref.at[block], block, line_send.at[0], device(line, side, 1 - core)).wait_recv()

    sent = []

    def send(source, block, sem, where):
        started = copy(source, block, sem, where)
        started.start()
        sent.append(started)

    for step in range(1, lines):
        send(mine_ref, me, line_send.at[step - 1], device((line + step) % lines, side, core))
    send(mine_ref, me, side_send.at[0], device(line, 1 - side, core))
    send(mine_ref, me, core_send.at[0], device(line, side, 1 - core))
    all_ref[me] = mine_ref[...]

    one_hot = one_hot_ref[...].astype(jnp.bfloat16)
    part = mine_ref.shape[1] // 2

    def spread_rows(which, column):
        values = modulation_ref[which, :, column : column + part]
        high = values.astype(jnp.bfloat16)
        rest = values - high.astype(jnp.float32)
        low = rest.astype(jnp.bfloat16)
        lowest = (rest - low.astype(jnp.float32)).astype(jnp.bfloat16)
        total = jnp.dot(one_hot, lowest, preferred_element_type=jnp.float32)
        total = total + jnp.dot(one_hot, low, preferred_element_type=jnp.float32)
        return total + jnp.dot(one_hot, high, preferred_element_type=jnp.float32)

    for which in range(3):
        for column in range(0, rows_ref.shape[2], part):
            rows_ref[which, :, column : column + part] = spread_rows(which, column)

    half_rows = mine_ref.shape[0] // 2
    width = 2 * mine_ref.shape[1]
    own = mine_ref[...].astype(jnp.float32)
    first, second = own[:half_rows], own[half_rows:]
    own_mean = (
        jnp.sum(first, axis=1, keepdims=True) + jnp.sum(second, axis=1, keepdims=True)
    ) / width
    first, second = first - own_mean, second - own_mean
    variance = (
        jnp.sum(first * first, axis=1, keepdims=True)
        + jnp.sum(second * second, axis=1, keepdims=True)
    ) / width
    stats_ref[:half_rows] = jnp.broadcast_to(own_mean, (half_rows, 128))
    stats_ref[half_rows:] = jnp.broadcast_to(lax.rsqrt(variance + EPSILON), (half_rows, 128))

    for step in range(1, lines):
        block = (((line - step + lines) % lines) * 2 + side) * 2 + core
        arrived(block)
        send(all_ref.at[block], block, side_send.at[step], device(line, 1 - side, core))
        send(all_ref.at[block], block, core_send.at[step], device(line, side, 1 - core))
    for step in range(lines):
        block = (((line - step + lines) % lines) * 2 + 1 - side) * 2 + core
        arrived(block)
        send(all_ref.at[block], block, core_send.at[lines + step], device(line, side, 1 - core))
    for step in range(lines):
        for other in range(2):
            arrived((((line - step + lines) % lines) * 2 + other) * 2 + 1 - core)
    for started in sent:
        started.wait_send()

    n, block_rows, half = all_ref.shape
    total_rows, features = tokens_ref.shape
    width = half // 2
    flat = all_ref[...].reshape(n * block_rows, half)

    def picked(which, column):
        place = column % half
        return jnp.dot(
            pick_ref[2 * (column // half) + which],
            flat[:, place : place + width],
            preferred_element_type=jnp.float32,
        )

    def spread(which, column):
        return rows_ref[which, :, column : column + width]

    columns = range(0, features, width)
    total = jnp.zeros((total_rows, 1), jnp.float32)
    for column in columns:
        values = picked(0, column)
        tokens_ref[:, column : column + width] = values
        total = total + jnp.sum(values, axis=1, keepdims=True)
        gated = picked(1, column) * spread(2, column)
        gated_ref[:, column : column + width] = gated.astype(jnp.bfloat16)
    mean = total / features
    total = jnp.zeros((total_rows, 1), jnp.float32)
    for column in columns:
        centred = tokens_ref[:, column : column + width] - mean
        total = total + jnp.sum(centred * centred, axis=1, keepdims=True)
    inverse_std = lax.rsqrt(total / features + EPSILON)
    for column in columns:
        normed = (tokens_ref[:, column : column + width] - mean) * inverse_std
        tokens_ref[:, column : column + width] = normed
        modulated = normed * (1.0 + spread(1, column)) + spread(0, column)
        modulated_ref[:, column : column + width] = modulated.astype(jnp.bfloat16)

    across_last = (((1,), (1,)), ((), ()))
    loads[0].wait()
    value = (
        lax.dot_general(
            modulated_ref[...],
            in_weight_ref[...],
            across_last,
            preferred_element_type=jnp.float32,
        )
        + bias_ref[...][None, :]
    )
    root = np.float32(np.sqrt(2.0 / np.pi))
    cubic = np.float32(0.044715)
    square = value * value
    bend = jnp.tanh(root * (value + cubic * (square * value)))
    activated_ref[...] = (value * (0.5 * (1.0 + bend))).astype(jnp.bfloat16)
    slope = 0.5 * (1.0 + bend) + (0.5 * value) * (1.0 - bend * bend) * (
        root * (1.0 + 3.0 * cubic * square)
    )
    loads[1].wait()
    act_grad = lax.dot_general(
        gated_ref[...], out_weight_ref[...], across_last, preferred_element_type=jnp.float32
    )
    hidden_ref[...] = (act_grad * slope).astype(jnp.bfloat16)
    for column in columns:
        partial = jnp.dot(
            hidden_ref[...],
            in_weight_ref[:, column : column + width],
            preferred_element_type=jnp.float32,
        )
        terms_ref[:total_rows, column : column + width] = partial.astype(jnp.bfloat16)
        terms_ref[total_rows:, column : column + width] = (
            partial * tokens_ref[:, column : column + width]
        ).astype(jnp.bfloat16)


def middle(block, pick, one_hot, modulation, in_weight, in_bias, out_weight, n):
    lines = n // 4
    total_rows = one_hot.shape[0]
    hidden, features = in_weight.shape
    vmem = pl.BlockSpec(memory_space=pltpu.VMEM)
    hbm = pl.BlockSpec(memory_space=pl.ANY)
    shapes = (
        (total_rows, features),
        (total_rows, features),
        (total_rows, hidden),
        (total_rows, hidden),
        (2 * total_rows, features),
    )
    return pl.pallas_call(
        functools.partial(middle_kernel, lines),
        out_shape=tuple(jax.ShapeDtypeStruct(shape, jnp.bfloat16) for shape in shapes)
        + (jax.ShapeDtypeStruct((block.shape[0], 128), jnp.float32),),
        in_specs=[vmem, vmem, vmem, vmem, hbm, vmem, hbm],
        out_specs=(vmem,) * 6,
        scratch_shapes=[
            pltpu.VMEM((n,) + block.shape, block.dtype),
            pltpu.VMEM((hidden, features), jnp.bfloat16),
            pltpu.VMEM((hidden, features), jnp.bfloat16),
            pltpu.VMEM((total_rows, features), jnp.float32),
            pltpu.VMEM((3, total_rows, features), jnp.float32),
            pltpu.SemaphoreType.DMA((lines,)),
            pltpu.SemaphoreType.DMA((lines,)),
            pltpu.SemaphoreType.DMA((2 * lines,)),
            pltpu.SemaphoreType.DMA((n,)),
            pltpu.SemaphoreType.DMA((2,)),
        ],
        compiler_params=pltpu.CompilerParams(
            collective_id=0, has_side_effects=True, vmem_limit_bytes=56 * 2**20
        ),
        name="gather_and_middle",
    )(
        block,
        pick,
        one_hot,
        modulation.transpose(1, 0, 2),
        in_weight,
        in_bias,
        out_weight,
    )


def reduce_kernel(
    lines,
    parts_ref,
    out_ref,
    from_core,
    to_side,
    from_side,
    to_line,
    from_line,
    core_send,
    core_recv,
    side_send,
    side_recv,
    line_send,
    line_recv,
):
    me, line, side, core = position(lines)
    greet(lines, line, side, core)
    sent = []

    def send(source, target, send_sem, recv_sem, where):
        started = pltpu.make_async_remote_copy(
            src_ref=source,
            dst_ref=target,
            send_sem=send_sem,
            recv_sem=recv_sem,
            device_id=where,
            device_id_type=MESH,
        )
        started.start()
        sent.append(started)
        return started

    order = [(line + step) % lines for step in list(range(1, lines)) + [0]]
    core_copies = {}
    for away in (1, 0):
        for step, place in enumerate(order):
            other = 1 - side if away else side
            slot = away * lines + step
            core_copies[slot] = send(
                parts_ref.at[1 - core, other, place],
                from_core.at[slot],
                core_send.at[slot],
                core_recv.at[slot],
                device(line, side, 1 - core),
            )
    side_copies = []
    for step, place in enumerate(order):
        slot = lines + step
        core_copies[slot].wait_recv()
        to_side[step] = (
            parts_ref[core, 1 - side, place].astype(jnp.float32)
            + from_core[slot].astype(jnp.float32)
        ).astype(jnp.bfloat16)
        side_copies.append(
            send(
                to_side.at[step],
                from_side.at[step],
                side_send.at[step],
                side_recv.at[step],
                device(line, 1 - side, core),
            )
        )
    line_copies = []
    for step, place in enumerate(order):
        core_copies[step].wait_recv()
        side_copies[step].wait_recv()
        total = (
            parts_ref[core, side, place].astype(jnp.float32)
            + from_core[step].astype(jnp.float32)
            + from_side[step].astype(jnp.float32)
        )
        if step < lines - 1:
            to_line[step] = total.astype(jnp.bfloat16)
            line_copies.append(
                send(
                    to_line.at[step],
                    from_line.at[step],
                    line_send.at[step],
                    line_recv.at[step],
                    device(place, side, core),
                )
            )
        else:
            out_ref[...] = total
    for step in range(lines - 1):
        line_copies[step].wait_recv()
        out_ref[...] += from_line[step].astype(jnp.float32)
    for started in sent:
        started.wait_send()


def reduce_blocks(parts, n):
    lines = n // 4
    block = parts.shape[3:]
    return pl.pallas_call(
        functools.partial(reduce_kernel, lines),
        out_shape=jax.ShapeDtypeStruct(block, jnp.float32),
        in_specs=[pl.BlockSpec(memory_space=pltpu.VMEM)],
        out_specs=pl.BlockSpec(memory_space=pltpu.VMEM),
        scratch_shapes=[
            pltpu.VMEM((2 * lines,) + block, jnp.bfloat16),
            pltpu.VMEM((lines,) + block, jnp.bfloat16),
            pltpu.VMEM((lines,) + block, jnp.bfloat16),
            pltpu.VMEM((lines,) + block, jnp.bfloat16),
            pltpu.VMEM((lines,) + block, jnp.bfloat16),
            pltpu.SemaphoreType.DMA((2 * lines,)),
            pltpu.SemaphoreType.DMA((2 * lines,)),
            pltpu.SemaphoreType.DMA((lines,)),
            pltpu.SemaphoreType.DMA((lines,)),
            pltpu.SemaphoreType.DMA((lines,)),
            pltpu.SemaphoreType.DMA((lines,)),
        ],
        compiler_params=pltpu.CompilerParams(
            collective_id=1, has_side_effects=True, vmem_limit_bytes=20 * 2**20
        ),
        name="reduce_rows",
    )(parts)


def product_kernel(activated_ref, gated_ref, hidden_ref, modulated_ref, out_ref, in_ref):
    for left_ref, right_ref, target_ref in (
        (activated_ref, gated_ref, out_ref),
        (hidden_ref, modulated_ref, in_ref),
    ):
        target_ref[...] = lax.dot_general(
            left_ref[...],
            right_ref[...],
            (((0,), (0,)), ((), ())),
            preferred_element_type=jnp.float32,
        ).astype(jnp.bfloat16)


def weight_products(activated, gated_grad, hidden_grad, modulated):
    (total_rows, hidden), features = activated.shape, modulated.shape[1]
    width = 512
    left = pl.BlockSpec((total_rows, hidden), lambda index: (0, 0))
    right = pl.BlockSpec((total_rows, width), lambda index: (0, index))
    target = pl.BlockSpec((hidden, width), lambda index: (0, index))
    shape = jax.ShapeDtypeStruct((hidden, features), jnp.bfloat16)
    return pl.pallas_call(
        product_kernel,
        grid=(features // width,),
        out_shape=(shape, shape),
        in_specs=[left, right, left, right],
        out_specs=(target, target),
        compiler_params=pltpu.CompilerParams(vmem_limit_bytes=24 * 2**20),
        name="weight_products",
    )(activated, gated_grad, hidden_grad, modulated)


def finish(mod_grad, normed, inverse_std, scale, out_grad):
    normed_grad = mod_grad * (1.0 + scale)
    mean_grad = jnp.mean(normed_grad, axis=1, keepdims=True)
    mean_proj = jnp.mean(normed_grad * normed, axis=1, keepdims=True)
    result = (
        out_grad.astype(jnp.float32) + (normed_grad - mean_grad - normed * mean_proj) * inverse_std
    )
    return result.astype(jnp.bfloat16)


def per_device(
    tokens, out_grad, ffn_out, modulation, in_weight, in_bias, out_weight, frame_ids, frame_slot
):
    rows, features = tokens.shape
    frame_count = modulation.shape[0]
    n = lax.axis_size("seq")
    lines = n // 4
    total_rows = rows * n
    half = features // 2
    row_base = lax.axis_index("seq") * rows

    one_hot = frame_ids[:, None] == jnp.arange(frame_count, dtype=jnp.int32)[None, :]
    row_slot = jnp.sum(jnp.where(one_hot, frame_slot[None, :], 0), axis=1)
    one_hot = one_hot.astype(jnp.float32)

    mine = jnp.concatenate([tokens[:, :half], out_grad[:, :half], tokens[:, half:], out_grad[:, half:]], axis=0)
    source = np.arange(total_rows) // rows * 4 * rows + np.arange(total_rows) % rows
    pick = np.stack([source + kind * rows for kind in range(4)])[:, :, None]
    pick = jnp.asarray(pick == np.arange(4 * total_rows), jnp.bfloat16)
    modulated, gated_grad, activated, hidden_grad, terms, stats = middle(
        mine, pick, one_hot, modulation, in_weight.T, in_bias, out_weight, n
    )

    per_owner = (frame_count + n - 1) // n
    kinds = rows + 3 * per_owner
    kinds += kinds % 2
    owner = np.arange(n).reshape(lines, 2, 2).transpose(2, 1, 0).reshape(n, 1)
    token_of = np.full((n, kinds), -1, np.int32)
    token_of[:, :rows] = owner * rows + np.arange(rows)
    slot_of = np.full((3, n, kinds), -1, np.int32)
    for kind in range(3):
        first = rows + kind * per_owner
        slot_of[kind, :, first : first + per_owner] = owner * per_owner + np.arange(per_owner)
    token_of = token_of.reshape(-1, 1)
    slot_of = slot_of.reshape(3, -1, 1)
    my_slot = lax.dynamic_slice_in_dim(row_slot, row_base, rows, 0)
    choose = jnp.concatenate(
        [
            (token_of == np.arange(total_rows, dtype=np.int32)[None, :])
            | (slot_of[0] == row_slot[None, :]),
            slot_of[1] == row_slot[None, :],
            slot_of[2] == my_slot[None, :],
        ],
        axis=1,
    ).astype(jnp.bfloat16)
    gate_rows = out_grad.astype(jnp.float32) * ffn_out.astype(jnp.float32)
    terms = jnp.concatenate(
        [
            terms,
            gate_rows.astype(jnp.bfloat16),
        ],
        axis=0,
    )
    parts = jnp.dot(choose, terms, preferred_element_type=jnp.float32).astype(jnp.bfloat16)
    cuts = 8
    parts = parts.reshape(2, 2, lines, kinds, cuts, features // cuts).transpose(0, 1, 2, 4, 3, 5)
    parts = parts.reshape(2, 2, lines, cuts * kinds, features // cuts)
    sums = reduce_blocks(parts, n)
    sums = sums.reshape(cuts, kinds, features // cuts).transpose(1, 0, 2).reshape(kinds, features)

    out_weight_grad, in_weight_grad = weight_products(activated, gated_grad, hidden_grad, modulated)
    in_weight_grad = in_weight_grad.T

    mod_grad = sums[:rows]
    my_hot = lax.dynamic_slice_in_dim(one_hot, row_base, rows, 0)
    my_scale = jnp.dot(my_hot, modulation[:, 1, :], precision=lax.Precision.HIGHEST)
    my_inverse_std = stats[2 * rows : 3 * rows, :1]
    my_normed = (tokens.astype(jnp.float32) - stats[:rows, :1]) * my_inverse_std
    token_grad = finish(mod_grad, my_normed, my_inverse_std, my_scale, out_grad)
    frame_grads = sums[rows : rows + 3 * per_owner].reshape(3, per_owner, features)
    return (token_grad, in_weight_grad, out_weight_grad, frame_grads.transpose(1, 0, 2))


def solution(mesh):
    in_specs = (
        P(("groups", "seq"), None),
        P(("groups", "seq"), None),
        P(("groups", "seq"), None),
        P("groups", None, None),
        P(None, "seq"),
        P("seq"),
        P("seq", None),
        P("groups"),
        P("groups"),
    )
    out_specs = (
        P(("groups", "seq"), None),
        P("groups", "seq"),
        P(("groups", "seq"), None),
        P(("groups", "seq"), None, None),
    )
    return jax.shard_map(
        per_device, mesh=mesh, in_specs=in_specs, out_specs=out_specs, check_vma=False
    )
```
